1024 devices in a mesh: wide: 64 (over z, x), narrow: 16 (over y, core).
Axes of the slice: x: 4, y: 8, z: 16, core: 2. Of those that a mesh axis runs over, the one named last changes fastest.
Arguments:
- amplitudes: float32 [960, 72000], P('narrow', 'wide'), may hold values from -6 to 6
- integrals: float32 [72000, 7680], P('wide', 'narrow'), may hold values from -0.0234375 to 0.0234375
- occupied_energy: float32 [60], replicated, may hold values from -3 to -1
- virtual_energy_rows: float32 [16], replicated, may hold values from 0.2 to 1.2
- virtual_energy_cols: float32 [128], replicated, may hold values from 0.2 to 1.2
Outputs:
- amplitude_step: float32 [960, 7680], P('wide', 'narrow')
The draws below stay inside these ranges and needn't reach their ends.
All inputs are finite; a program needn't handle non-finite values.
Results may differ from the reference program's by a relative error of at most 0.00012.
Values sent between devices are 32-bit elements; how exact they have to be, the bound alone decides.
No kernel may reach another device: no remote copies, remote signals or barrier semaphores. Data moves between devices by JAX's collectives and lax.ppermute only.
A program may use at most 32 MiB of HBM per device.

```python
import jax
import jax.numpy as jnp
from jax import lax

O = 60
AB = 16
BB = 128
KPAIRS = 72000
ROWS = 960
COLS = 7680


def block_scale(own_key, extent, pieces, smallest, top_value):
    def one(dim, blocks):
        draws = jax.random.uniform(jax.random.fold_in(jax.random.fold_in(own_key, 6), dim), (blocks,), jnp.float32, smallest / len(pieces), top_value / len(pieces))
        return jnp.repeat(jnp.exp(draws), extent[dim] // blocks).reshape((-1,) + (1,) * (len(extent) - dim - 1))

    loudness = one(*pieces[0])
    for cut in pieces[1:]:
        loudness = loudness * one(*cut)
    return loudness


def centred(key, dims, scale, bound, pieces=(), held_as=jnp.bfloat16):
    values = scale * jax.random.normal(key, dims, jnp.float32)
    if pieces:
        values = values * block_scale(key, dims, pieces, -0.22, 0.18)
    return jnp.clip(values, -bound, bound).astype(held_as)


def setup_inputs(seed: int = 0) -> dict:
    arg_keys = jax.random.split(jax.random.key(seed), 6)
    return {
        "amplitudes": centred(arg_keys[0], (ROWS, KPAIRS), 1.0, 6.0, ((0, 16), (1, 64)), jnp.float32),
        "integrals": centred(arg_keys[1], (KPAIRS, COLS), KPAIRS ** -0.5, 0.0234375, ((0, 64), (1, 16)), jnp.float32),
        "occupied_energy": jnp.clip(jax.random.uniform(arg_keys[2], (O,), jnp.float32, -3.0, -1.0), -3.0, -1.0),
        "virtual_energy_rows": jnp.clip(jax.random.uniform(arg_keys[3], (AB,), jnp.float32, 0.2, 1.2), 0.2, 1.2),
        "virtual_energy_cols": jnp.clip(jax.random.uniform(arg_keys[4], (BB,), jnp.float32, 0.2, 1.2), 0.2, 1.2),
    }


def reference(amplitudes, integrals, occupied_energy, virtual_energy_rows, virtual_energy_cols):
    cycle_term = jnp.dot(amplitudes, integrals, precision=lax.Precision.HIGHEST, preferred_element_type=jnp.float32)
    row_energy = (occupied_energy[None, :] - virtual_energy_rows[:, None]).reshape(-1)
    col_energy = (occupied_energy[None, :] - virtual_energy_cols[:, None]).reshape(-1)
    denominator = row_energy[:, None] + col_energy[None, :]
    return cycle_term / denominator
```

```python
import jax
import jax.numpy as jnp
from jax import lax
from jax.sharding import PartitionSpec as P

Z, X, Y, CORES = 16, 4, 8, 2
AXES = ("wide", "narrow")
OFFSETS = (0, 2, 1, 4, 3, 6, 5, 8)


def table(move):
    def index(z, x, y, c):
        return (z % Z * X + x % X) * (Y * CORES) + y % Y * CORES + c

    return [
        (index(z, x, y, c), index(*move(z, x, y, c)))
        for z in range(Z)
        for x in range(X)
        for y in range(Y)
        for c in range(CORES)
    ]


def send(array, move):
    return lax.ppermute(array, AXES, table(move))


def other_core(z, x, y, c):
    return z, x, y, 1 - c


def along_y(z, x, y, c):
    return z, x, y + (1 if c == 0 else -1), c


def along_x(step):
    return lambda z, x, y, c: (z, x + step, y, c)


def to_z(u, y, c):
    return 2 * y - u if c == 0 else 2 * y + 1 + u


def from_z(z, y, c):
    return (2 * y - z) % Z if c == 0 else (z - 2 * y - 1) % Z


def along_u(step):
    return lambda z, x, y, c: (to_z(from_z(z, y, c) + step, y, c), x, y, c)


def final(turn):
    def move(z, x, y, c):
        u = from_z(z, y, c)
        piece = (u // 4 + turn) % 4
        number = u % 4 * 4 + piece
        offset, half = OFFSETS[number // 2], number % 2
        return to_z(offset, y, c), x, y, c if half == 0 else 1 - c

    return move


def per_device(amplitudes, integrals, occupied_energy, virtual_energy_rows, virtual_energy_cols):
    wide, narrow = lax.axis_index("wide"), lax.axis_index("narrow")
    z, x, y, c = wide // X, wide % X, narrow // CORES, narrow % CORES
    u = jnp.where(c == 0, 2 * y - z, z - 2 * y - 1) % Z
    rows, depth = amplitudes.shape
    cols = integrals.shape[1]
    share = rows // X

    block = jnp.pad(amplitudes.reshape(X, share, depth), ((0, 0), (0, 16 - share), (0, 0)))
    block = jnp.roll(block, -x, axis=0).reshape(X * 16, depth)
    swapped = send(block, other_core)
    others = send(integrals, other_core)
    a1 = send(block, along_y)
    b1 = send(swapped, along_y)
    a2 = send(a1, along_y)
    b2 = send(b1, along_y)
    a3 = send(a2, along_y)
    b3 = send(b2, along_y)
    a4 = send(a3, along_y)

    def partial_sums(blocks):
        tall = jnp.concatenate(blocks, 0)
        halves = [
            jnp.dot(tall, part, precision=lax.Precision.HIGH, preferred_element_type=jnp.float32)
            for part in (integrals, others)
        ]
        return [half.reshape(len(blocks), X, 16, cols) for half in halves]

    def sum_over_x(blocks):
        halves = jnp.stack(partial_sums(blocks), 1)
        total = halves[:, :, 0]
        for place, step in ((1, 1), (3, -1), (2, 2)):
            total = total + send(halves[:, :, place], along_x(step))
        return total

    groups = ((block, a1, b1, a2, b2), (a3, b3, a4))
    pieces = jnp.concatenate([sum_over_x(blocks) for blocks in groups], 0).reshape(4, 4, 16, cols)

    mine = u % 4
    total = lax.dynamic_index_in_dim(pieces, mine, 0, keepdims=False)
    for step in (1, -1, 2):
        total = total + send(lax.dynamic_index_in_dim(pieces, (mine + step) % 4, 0, keepdims=False), along_u(step))
    cycle_term = None
    for turn in range(4):
        part = send(lax.dynamic_index_in_dim(total, (u // 4 + turn) % 4, 0, keepdims=False), final(turn))
        cycle_term = part if cycle_term is None else cycle_term + part
    cycle_term = cycle_term[:share]

    row_energy = (occupied_energy[None, :] - virtual_energy_rows[:, None]).reshape(-1)
    col_energy = (occupied_energy[None, :] - virtual_energy_cols[:, None]).reshape(-1)
    row_part = lax.dynamic_slice_in_dim(row_energy, wide * share, share)
    col_part = lax.dynamic_slice_in_dim(col_energy, narrow * cols, cols)
    return cycle_term / (row_part[:, None] + col_part[None, :])


def solution(mesh):
    in_specs = (P("narrow", "wide"), P("wide", "narrow"), P(), P(), P())
    out_specs = P("wide", "narrow")
    return jax.shard_map(
        per_device, mesh=mesh, in_specs=in_specs, out_specs=out_specs, check_vma=False
    )
```

```python
import jax
import jax.numpy as jnp
from jax import lax
from jax.sharding import PartitionSpec as P

Z, X, Y, CORES = 16, 4, 8, 2
AXES = ("wide", "narrow")
EVEN, ODD = (0, -2, -4, 2), (-1, 1, -3, 3)


def device(z, x, y, c):
    return (z % Z * X + x % X) * (Y * CORES) + y % Y * CORES + c


def table(move):
    return [
        (device(z, x, y, c), device(*move(z, x, y, c)))
        for z in range(Z)
        for x in range(X)
        for y in range(Y)
        for c in range(CORES)
    ]


def send(array, move):
    return lax.ppermute(array, AXES, table(move))


def other_core(z, x, y, c):
    return z, x, y, 1 - c


def along_y(step):
    return lambda z, x, y, c: (z, x, y + (step if c == 0 else -step), c)


def along_x(step):
    return lambda z, x, y, c: (z, x + step, y, c)


def far_step(z):
    return z % 4 // 2 * 4 - 2


def to_window(near, core):
    def move(z, x, y, c):
        if z % 2 == c:
            return (z if near else z + far_step(z)), x, y, 1 - core
        return (z + 1 if near else z - 1), x, y, core

    return move


def classes():
    groups = []
    for r in range(4):
        c = r % 2
        for x in range(X):
            for y in range(Y):
                offsets = EVEN if (2 * y + c) % 4 == r else ODD
                places = [2 * (y + (o if c == 0 else -o)) + c for o in offsets]
                for core in range(CORES):
                    groups.append([device(z, x, y, core) for z in places])
    return groups


def per_device(amplitudes, integrals, occupied_energy, virtual_energy_rows, virtual_energy_cols):
    wide, narrow = lax.axis_index("wide"), lax.axis_index("narrow")
    z, x, y, c = wide // X, wide % X, narrow // CORES, narrow % CORES
    rows, depth = amplitudes.shape
    cols = integrals.shape[1]
    share = rows // X

    block = jnp.pad(amplitudes.reshape(X, share, depth), ((0, 0), (0, 16 - share), (0, 0)))
    block = jnp.roll(block, -x, axis=0).reshape(X * 16, depth)
    f1 = send(block, along_y(1))
    h1 = send(block, along_y(-1))
    others = send(integrals, other_core)
    f2 = send(f1, along_y(1))
    h2 = send(h1, along_y(-1))

    def messages(blocks):
        tall = jnp.concatenate(blocks, 0)
        halves = [
            jnp.dot(tall, part, precision=lax.Precision.HIGH, preferred_element_type=jnp.float32)
            for part in (integrals, others)
        ]
        halves = jnp.stack([half.reshape(len(blocks), X, 16, cols) for half in halves], 1)
        return [halves[:, :, place] for place in range(X)]

    def sum_over_x(parts):
        return parts[0] + send(parts[1], along_x(1)) + send(parts[3], along_x(-1)) + send(parts[2], along_x(2))

    f2, others = lax.optimization_barrier((f2, others))
    f3 = send(f2, along_y(1))
    h3 = send(h2, along_y(-1))
    early = messages((block, f1, h1, f2, h2))
    f3, early = lax.optimization_barrier((f3, early))
    f4 = send(f3, along_y(1))
    first = sum_over_x(early)
    second = sum_over_x(messages((f3, h3, f4)))
    pieces = jnp.stack(
        [first[0], first[3], second[2], first[4], first[1], first[2], second[0], second[1]], 1
    )
    pieces = pieces.reshape(2, 2, 4, 16, cols)

    at_home = z % 2 == c
    total = 0.0
    for near in (True, False):
        place = jnp.where(at_home, z if near else z + 2, z + 1 if near else z - 1) % 4
        odd = (place != (2 * y + c) % 4).astype(jnp.int32)
        for core in range(CORES):
            half = (jnp.where(at_home, 1 - core, core) != c).astype(jnp.int32)
            part = lax.dynamic_slice(pieces, (half, odd, 0, 0, 0), (1, 1, 4, 16, cols))
            total = total + send(part.reshape(4, 16, cols), to_window(near, core))
    spread = lax.all_to_all(total, AXES, 0, 0, tiled=True, axis_index_groups=classes())
    cycle_term = spread[0] + spread[1] + spread[2] + spread[3]
    cycle_term = cycle_term[:share]

    row_energy = (occupied_energy[None, :] - virtual_energy_rows[:, None]).reshape(-1)
    col_energy = (occupied_energy[None, :] - virtual_energy_cols[:, None]).reshape(-1)
    row_part = lax.dynamic_slice_in_dim(row_energy, wide * share, share)
    col_part = lax.dynamic_slice_in_dim(col_energy, narrow * cols, cols)
    return cycle_term / (row_part[:, None] + col_part[None, :])


def solution(mesh):
    in_specs = (P("narrow", "wide"), P("wide", "narrow"), P(), P(), P())
    out_specs = P("wide", "narrow")
    return jax.shard_map(
        per_device, mesh=mesh, in_specs=in_specs, out_specs=out_specs, check_vma=False
    )
```

```python
import jax
import jax.numpy as jnp
from jax import lax
from jax.sharding import PartitionSpec as P

Z, X, Y, CORES = 16, 4, 8, 2
AXES = ("wide", "narrow")
EVEN, ODD = (0, -2, -4, 2), (-1, 1, -3, 3)


def device(z, x, y, c):
    return (z % Z * X + x % X) * (Y * CORES) + y % Y * CORES + c


def table(move):
    return [
        (device(z, x, y, c), device(*move(z, x, y, c)))
        for z in range(Z)
        for x in range(X)
        for y in range(Y)
        for c in range(CORES)
    ]


def send(array, move):
    return lax.ppermute(array, AXES, table(move))


def other_core(z, x, y, c):
    return z, x, y, 1 - c


def along_y(step):
    return lambda z, x, y, c: (z, x, y + (step if c == 0 else -step), c)


def swap_z(first):
    def move(z, x, y, c):
        return z + (1 if (z % 2 == 0) == (first == (c == 0)) else -1), x, y, c

    return move


def planes():
    return [
        [device(z, x, y, c) for x in range(X) for c in range(CORES)] for z in range(Z) for y in range(Y)
    ]


def classes():
    groups = []
    for r in range(4):
        c = r % 2
        for x in range(X):
            for y in range(Y):
                offsets = EVEN if (2 * y + c) % 4 == r else ODD
                places = [2 * (y + (o if c == 0 else -o)) + c for o in offsets]
                for core in range(CORES):
                    groups.append([device(z, x, y, core) for z in places])
    return groups


def per_device(amplitudes, integrals, occupied_energy, virtual_energy_rows, virtual_energy_cols):
    wide, narrow = lax.axis_index("wide"), lax.axis_index("narrow")
    z, y, c = wide // X, narrow // CORES, narrow % CORES
    rows, depth = amplitudes.shape
    cols = integrals.shape[1]
    share = rows // X

    block = jnp.pad(amplitudes.reshape(X, share, depth), ((0, 0), (0, 16 - share), (0, 0)))
    block = block.reshape(X * 16, depth)
    block, integrals = lax.optimization_barrier((block, integrals))
    f1 = send(block, along_y(1))
    h1 = send(block, along_y(-1))
    others = send(integrals, other_core)
    f2 = send(f1, along_y(1))
    h2 = send(h1, along_y(-1))

    def sums_over_x(blocks):
        tall = jnp.concatenate(blocks, 0)
        own, other = (
            jnp.dot(tall, part, precision=lax.Precision.HIGH, preferred_element_type=jnp.float32).reshape(
                len(blocks), X, 16, cols
            )
            for part in (integrals, others)
        )
        halves = jnp.stack([jnp.where(c == 0, own, other), jnp.where(c == 0, other, own)], 0)
        return halves.transpose(2, 0, 1, 3, 4).reshape(X * CORES, len(blocks), 16, cols)

    def exchange_x(parts):
        parts = lax.all_to_all(parts, AXES, 0, 0, tiled=True, axis_index_groups=planes())
        return parts.reshape(X, CORES, *parts.shape[1:]).sum(0)

    f2, h2, others = lax.optimization_barrier((f2, h2, others))
    h3 = send(h2, along_y(-1))
    f3 = send(f2, along_y(1))
    early = sums_over_x((block, f1, h1, f2, h2))
    f3, early = lax.optimization_barrier((f3, early))
    f4 = send(f3, along_y(1))
    first = exchange_x(early)
    late = sums_over_x((f3, h3, f4))
    first, late = lax.optimization_barrier((first, late))
    second = exchange_x(late)
    even = jnp.stack([first[:, 0], first[:, 3], second[:, 2], first[:, 4]], 1)
    odd = jnp.stack([first[:, 1], first[:, 2], second[:, 0], second[:, 1]], 1)
    pieces = jnp.concatenate([even, odd], 0)

    def class_of(place):
        return lax.dynamic_index_in_dim(pieces, (place - 2 * y) % 4, 0, keepdims=False)

    one = jnp.where((z % 2 == 0) == (c == 0), 1, -1)
    sent = jnp.stack([class_of(z + one), class_of(z + 2 * one)], 0)
    kept = jnp.stack([class_of(z), class_of(z - one)], 0)
    kept = kept + send(sent, swap_z(True))
    total = kept[0] + send(kept[1], swap_z(False))
    spread = lax.all_to_all(total, AXES, 0, 0, tiled=True, axis_index_groups=classes())
    cycle_term = spread[0] + spread[1] + spread[2] + spread[3]
    cycle_term = cycle_term[:share]

    row_energy = (occupied_energy[None, :] - virtual_energy_rows[:, None]).reshape(-1)
    col_energy = (occupied_energy[None, :] - virtual_energy_cols[:, None]).reshape(-1)
    row_part = lax.dynamic_slice_in_dim(row_energy, wide * share, share)
    col_part = lax.dynamic_slice_in_dim(col_energy, narrow * cols, cols)
    return cycle_term / (row_part[:, None] + col_part[None, :])


def solution(mesh):
    in_specs = (P("narrow", "wide"), P("wide", "narrow"), P(), P(), P())
    out_specs = P("wide", "narrow")
    return jax.shard_map(
        per_device, mesh=mesh, in_specs=in_specs, out_specs=out_specs, check_vma=False
    )
```

```python
import jax
import jax.numpy as jnp
from jax import lax
from jax.sharding import PartitionSpec as P

Z, X, Y, CORES = 16, 4, 8, 2
AXES = ("wide", "narrow")
EVEN, ODD = (0, -2, -4, 2), (-1, 1, -3, 3)


def device(z, x, y, c):
    return (z % Z * X + x % X) * (Y * CORES) + y % Y * CORES + c


def table(move):
    return [
        (device(z, x, y, c), device(*move(z, x, y, c)))
        for z in range(Z)
        for x in range(X)
        for y in range(Y)
        for c in range(CORES)
    ]


def send(array, move):
    return lax.ppermute(array, AXES, table(move))


def other_core(z, x, y, c):
    return z, x, y, 1 - c


def along_y(step):
    return lambda z, x, y, c: (z, x, y + (step if c == 0 else -step), c)


def along_x(step):
    return lambda z, x, y, c: (z, x + step, y, c)


def far_step(z):
    return z % 4 // 2 * 4 - 2


def to_window(near, core):
    def move(z, x, y, c):
        if z % 2 == c:
            return (z if near else z + far_step(z)), x, y, 1 - core
        return (z + 1 if near else z - 1), x, y, core

    return move


def classes():
    groups = []
    for r in range(4):
        c = r % 2
        for x in range(X):
            for y in range(Y):
                offsets = EVEN if (2 * y + c) % 4 == r else ODD
                places = [2 * (y + (o if c == 0 else -o)) + c for o in offsets]
                for core in range(CORES):
                    groups.append([device(z, x, y, core) for z in places])
    return groups


def per_device(amplitudes, integrals, occupied_energy, virtual_energy_rows, virtual_energy_cols):
    wide, narrow = lax.axis_index("wide"), lax.axis_index("narrow")
    z, x, y, c = wide // X, wide % X, narrow // CORES, narrow % CORES
    rows, depth = amplitudes.shape
    cols = integrals.shape[1]
    share = rows // X

    block = jnp.pad(amplitudes.reshape(X, share, depth), ((0, 0), (0, 16 - share), (0, 0)))
    block = jnp.roll(block, -x, axis=0).reshape(X * 16, depth)
    f1 = send(block, along_y(1))
    block_after, occupied_energy = lax.optimization_barrier((block, occupied_energy))
    row_energy = (occupied_energy[None, :] - virtual_energy_rows[:, None]).reshape(-1)
    col_energy = (occupied_energy[None, :] - virtual_energy_cols[:, None]).reshape(-1)
    row_part = lax.dynamic_slice_in_dim(row_energy, wide * share, share)
    col_part = lax.dynamic_slice_in_dim(col_energy, narrow * cols, cols)
    denominator = row_part[:, None] + col_part[None, :]
    block_after, denominator = lax.optimization_barrier((block_after, denominator))
    h1 = send(block_after, along_y(-1))
    others = send(integrals, other_core)
    f2 = send(f1, along_y(1))
    nearest = jnp.concatenate([block, f1], 0)
    h1_after, nearest = lax.optimization_barrier((h1, nearest))
    h2 = send(h1_after, along_y(-1))

    def messages(tall):
        halves = [
            jnp.dot(tall, part, precision=lax.Precision.HIGH, preferred_element_type=jnp.float32)
            for part in (integrals, others)
        ]
        halves = jnp.stack([half.reshape(-1, X, 16, cols) for half in halves], 1)
        return [halves[:, :, place] for place in range(X)]

    def sum_over_x(parts):
        return parts[0] + send(parts[1], along_x(1)) + send(parts[3], along_x(-1)) + send(parts[2], along_x(2))

    f2, others = lax.optimization_barrier((f2, others))
    f3 = send(f2, along_y(1))
    h2_after, _ = lax.optimization_barrier((h2, f2))
    h3 = send(h2_after, along_y(-1))
    early = messages(jnp.concatenate([nearest, h1, f2, h2], 0))
    f3, early = lax.optimization_barrier((f3, early))
    f4 = send(f3, along_y(1))
    first = sum_over_x(early)
    second = sum_over_x(messages(jnp.concatenate([f3, h3, f4], 0)))
    pieces = jnp.stack(
        [first[0], first[3], second[2], first[4], first[1], first[2], second[0], second[1]], 1
    )
    pieces = pieces.reshape(2, 2, 4, 16, cols)

    at_home = z % 2 == c
    total = 0.0
    for near in (True, False):
        place = jnp.where(at_home, z if near else z + 2, z + 1 if near else z - 1) % 4
        odd = (place != (2 * y + c) % 4).astype(jnp.int32)
        for core in range(CORES):
            half = (jnp.where(at_home, 1 - core, core) != c).astype(jnp.int32)
            part = lax.dynamic_slice(pieces, (half, odd, 0, 0, 0), (1, 1, 4, 16, cols))
            total = total + send(part.reshape(4, 16, cols), to_window(near, core))
    spread = lax.all_to_all(total, AXES, 0, 0, tiled=True, axis_index_groups=classes())
    cycle_term = spread[0] + spread[1] + spread[2] + spread[3]
    cycle_term = cycle_term[:share]

    return cycle_term / denominator


def solution(mesh):
    in_specs = (P("narrow", "wide"), P("wide", "narrow"), P(), P(), P())
    out_specs = P("wide", "narrow")
    return jax.shard_map(
        per_device, mesh=mesh, in_specs=in_specs, out_specs=out_specs, check_vma=False
    )
```

```python
import jax
import jax.numpy as jnp
from jax import lax
from jax.sharding import PartitionSpec as P

Z, X, Y, CORES = 16, 4, 8, 2
AXES = ("wide", "narrow")
EVEN, ODD = (0, -2, -4, 2), (-1, 1, -3, 3)


def device(z, x, y, c):
    return (z % Z * X + x % X) * (Y * CORES) + y % Y * CORES + c


def table(move):
    return [
        (device(z, x, y, c), device(*move(z, x, y, c)))
        for z in range(Z)
        for x in range(X)
        for y in range(Y)
        for c in range(CORES)
    ]


def send(array, move):
    return lax.ppermute(array, AXES, table(move))


def other_core(z, x, y, c):
    return z, x, y, 1 - c


def along_y(step):
    return lambda z, x, y, c: (z, x, y + (step if c == 0 else -step), c)


def along_x(step):
    return lambda z, x, y, c: (z, x + step, y, c)


def far_step(z):
    return z % 4 // 2 * 4 - 2


def to_window(near, core):
    def move(z, x, y, c):
        if z % 2 == c:
            return (z if near else z + far_step(z)), x, y, 1 - core
        return (z + 1 if near else z - 1), x, y, core

    return move


def classes():
    groups = []
    for r in range(4):
        c = r % 2
        for x in range(X):
            for y in range(Y):
                offsets = EVEN if (2 * y + c) % 4 == r else ODD
                places = [2 * (y + (o if c == 0 else -o)) + c for o in offsets]
                for core in range(CORES):
                    groups.append([device(z, x, y, core) for z in places])
    return groups


def per_device(amplitudes, integrals, occupied_energy, virtual_energy_rows, virtual_energy_cols):
    wide, narrow = lax.axis_index("wide"), lax.axis_index("narrow")
    z, x, y, c = wide // X, wide % X, narrow // CORES, narrow % CORES
    rows, depth = amplitudes.shape
    cols = integrals.shape[1]
    share = rows // X

    block = jnp.pad(amplitudes.reshape(X, share, depth), ((0, 0), (0, 16 - share), (0, 0)))
    block = jnp.roll(block, -x, axis=0).reshape(X * 16, depth)
    f1 = send(block, along_y(1))
    h1 = send(block, along_y(-1))
    others = send(integrals, other_core)
    f2 = send(f1, along_y(1))
    h2 = send(h1, along_y(-1))

    def messages(blocks):
        tall = jnp.concatenate(blocks, 0)
        halves = [
            jnp.dot(tall, part, precision=lax.Precision.HIGH, preferred_element_type=jnp.float32)
            for part in (integrals, others)
        ]
        halves = jnp.stack([half.reshape(len(blocks), X, 16, cols) for half in halves], 1)
        return [halves[:, :, place] for place in range(X)]

    def sum_over_x(parts):
        return parts[0] + send(parts[1], along_x(1)) + send(parts[3], along_x(-1)) + send(parts[2], along_x(2))

    f3 = send(f2, along_y(1))
    h3 = send(h2, along_y(-1))
    early = messages((block, f1, h1, f2, h2))
    h3_after, early = lax.optimization_barrier((h3, early))
    h4 = send(h3_after, along_y(-1))
    first = sum_over_x(early)
    second = sum_over_x(messages((f3, h3, h4)))
    pieces = jnp.stack(
        [first[0], first[3], second[2], first[4], first[1], first[2], second[0], second[1]], 1
    )
    pieces = pieces.reshape(2, 2, 4, 16, cols)

    at_home = z % 2 == c
    total = 0.0
    for near in (True, False):
        place = jnp.where(at_home, z if near else z + 2, z + 1 if near else z - 1) % 4
        odd = (place != (2 * y + c) % 4).astype(jnp.int32)
        for core in range(CORES):
            half = (jnp.where(at_home, 1 - core, core) != c).astype(jnp.int32)
            part = lax.dynamic_slice(pieces, (half, odd, 0, 0, 0), (1, 1, 4, 16, cols))
            total = total + send(part.reshape(4, 16, cols), to_window(near, core))
    spread = lax.all_to_all(total, AXES, 0, 0, tiled=True, axis_index_groups=classes())
    cycle_term = spread[0] + spread[1] + spread[2] + spread[3]
    cycle_term = cycle_term[:share]

    row_energy = (occupied_energy[None, :] - virtual_energy_rows[:, None]).reshape(-1)
    col_energy = (occupied_energy[None, :] - virtual_energy_cols[:, None]).reshape(-1)
    row_part = lax.dynamic_slice_in_dim(row_energy, wide * share, share)
    col_part = lax.dynamic_slice_in_dim(col_energy, narrow * cols, cols)
    return cycle_term / (row_part[:, None] + col_part[None, :])


def solution(mesh):
    in_specs = (P("narrow", "wide"), P("wide", "narrow"), P(), P(), P())
    out_specs = P("wide", "narrow")
    return jax.shard_map(
        per_device, mesh=mesh, in_specs=in_specs, out_specs=out_specs, check_vma=False
    )
```

```python
import jax
import jax.numpy as jnp
from jax import lax
from jax.sharding import PartitionSpec as P

Z, X, Y, CORES = 16, 4, 8, 2
AXES = ("wide", "narrow")
EVEN, ODD = (0, -2, -4, 2), (-1, 1, -3, 3)


def device(z, x, y, c):
    return (z % Z * X + x % X) * (Y * CORES) + y % Y * CORES + c


def table(move):
    return [
        (device(z, x, y, c), device(*move(z, x, y, c)))
        for z in range(Z)
        for x in range(X)
        for y in range(Y)
        for c in range(CORES)
    ]


def send(array, move):
    return lax.ppermute(array, AXES, table(move))


def other_core(z, x, y, c):
    return z, x, y, 1 - c


def along_y(step):
    return lambda z, x, y, c: (z, x, y + (step if c == 0 else -step), c)


def side_of(x, c):
    return 1 if (x % 2 == 0) == (c == 0) else -1


def along_x(step):
    return lambda z, x, y, c: (z, x + step * side_of(x, c), y, c)


def far_step(z):
    return z % 4 // 2 * 4 - 2


def to_window(near, core):
    def move(z, x, y, c):
        if z % 2 == c:
            return (z if near else z + far_step(z)), x, y, 1 - core
        return (z + 1 if near else z - 1), x, y, core

    return move


def classes():
    groups = []
    for r in range(4):
        c = r % 2
        for x in range(X):
            for y in range(Y):
                offsets = EVEN if (2 * y + c) % 4 == r else ODD
                places = [2 * (y + (o if c == 0 else -o)) + c for o in offsets]
                for core in range(CORES):
                    groups.append([device(z, x, y, core) for z in places])
    return groups


def per_device(amplitudes, integrals, occupied_energy, virtual_energy_rows, virtual_energy_cols):
    wide, narrow = lax.axis_index("wide"), lax.axis_index("narrow")
    z, x, y, c = wide // X, wide % X, narrow // CORES, narrow % CORES
    rows, depth = amplitudes.shape
    cols = integrals.shape[1]
    share = rows // X

    side = jnp.where((x % 2 == 0) == (c == 0), 1, -1)
    block = jnp.pad(amplitudes.reshape(X, share, depth), ((0, 0), (0, 16 - share), (0, 0)))
    block = jnp.concatenate(
        [lax.dynamic_index_in_dim(block, (x + side * k) % X, 0, keepdims=False) for k in range(X)], 0
    )
    f1 = send(block, along_y(1))
    h1 = send(block, along_y(-1))
    others = send(integrals, other_core)
    f2 = send(f1, along_y(1))
    h2 = send(h1, along_y(-1))

    def partial_sums(blocks):
        tall = jnp.concatenate(blocks, 0)
        halves = [
            jnp.dot(tall, part, precision=lax.Precision.HIGH, preferred_element_type=jnp.float32)
            for part in (integrals, others)
        ]
        return jnp.stack([half.reshape(len(blocks), X, 16, cols) for half in halves], 1)

    def halving_sum(parts):
        arrived = send(parts[:, :, 1:3], along_x(1))
        passed_on = parts[:, :, 3] + arrived[:, :, 1]
        return parts[:, :, 0] + arrived[:, :, 0] + send(passed_on, along_x(-1))

    def direct_sum(parts):
        return parts[:, :, 0] + send(parts[:, :, 1], along_x(1)) + send(parts[:, :, 3], along_x(-1)) + send(parts[:, :, 2], along_x(2))

    f3 = send(f2, along_y(1))
    h3 = send(h2, along_y(-1))
    early = partial_sums((block, f1, h1, f2, h2))
    f3_after, early = lax.optimization_barrier((f3, early))
    f4 = send(f3_after, along_y(1))
    first = halving_sum(early)
    second = direct_sum(partial_sums((f3, h3, f4)))
    pieces = jnp.stack(
        [first[0], first[3], second[2], first[4], first[1], first[2], second[0], second[1]], 1
    )
    pieces = pieces.reshape(2, 2, 4, 16, cols)

    at_home = z % 2 == c
    total = 0.0
    for near in (True, False):
        place = jnp.where(at_home, z if near else z + 2, z + 1 if near else z - 1) % 4
        odd = (place != (2 * y + c) % 4).astype(jnp.int32)
        for core in range(CORES):
            half = (jnp.where(at_home, 1 - core, core) != c).astype(jnp.int32)
            part = lax.dynamic_slice(pieces, (half, odd, 0, 0, 0), (1, 1, 4, 16, cols))
            total = total + send(part.reshape(4, 16, cols), to_window(near, core))
    spread = lax.all_to_all(total, AXES, 0, 0, tiled=True, axis_index_groups=classes())
    cycle_term = spread[0] + spread[1] + spread[2] + spread[3]
    cycle_term = cycle_term[:share]

    row_energy = (occupied_energy[None, :] - virtual_energy_rows[:, None]).reshape(-1)
    col_energy = (occupied_energy[None, :] - virtual_energy_cols[:, None]).reshape(-1)
    row_part = lax.dynamic_slice_in_dim(row_energy, wide * share, share)
    col_part = lax.dynamic_slice_in_dim(col_energy, narrow * cols, cols)
    return cycle_term / (row_part[:, None] + col_part[None, :])


def solution(mesh):
    in_specs = (P("narrow", "wide"), P("wide", "narrow"), P(), P(), P())
    out_specs = P("wide", "narrow")
    return jax.shard_map(
        per_device, mesh=mesh, in_specs=in_specs, out_specs=out_specs, check_vma=False
    )
```

```python
import jax
import jax.numpy as jnp
from jax import lax
from jax.sharding import PartitionSpec as P

Z, X, Y, CORES = 16, 4, 8, 2
AXES = ("wide", "narrow")
EVEN, ODD = (0, -2, -4, 2), (-1, 1, -3, 3)


def device(z, x, y, c):
    return (z % Z * X + x % X) * (Y * CORES) + y % Y * CORES + c


def table(move):
    return [
        (device(z, x, y, c), device(*move(z, x, y, c)))
        for z in range(Z)
        for x in range(X)
        for y in range(Y)
        for c in range(CORES)
    ]


def send(array, move):
    return lax.ppermute(array, AXES, table(move))


def other_core(z, x, y, c):
    return z, x, y, 1 - c


def along_y(step):
    return lambda z, x, y, c: (z, x, y + (step if c == 0 else -step), c)


def side_of(x, c):
    return 1 if (x % 2 == 0) == (c == 0) else -1


def along_x(step):
    return lambda z, x, y, c: (z, x + step * side_of(x, c), y, c)


def far_step(z):
    return z % 4 // 2 * 4 - 2


def to_window(near, core):
    def move(z, x, y, c):
        if z % 2 == c:
            return (z if near else z + far_step(z)), x, y, 1 - core
        return (z + 1 if near else z - 1), x, y, core

    return move


def classes():
    groups = []
    for r in range(4):
        c = r % 2
        for x in range(X):
            for y in range(Y):
                offsets = EVEN if (2 * y + c) % 4 == r else ODD
                places = [2 * (y + (o if c == 0 else -o)) + c for o in offsets]
                for core in range(CORES):
                    groups.append([device(z, x, y, core) for z in places])
    return groups


def per_device(amplitudes, integrals, occupied_energy, virtual_energy_rows, virtual_energy_cols):
    wide, narrow = lax.axis_index("wide"), lax.axis_index("narrow")
    z, x, y, c = wide // X, wide % X, narrow // CORES, narrow % CORES
    rows, depth = amplitudes.shape
    cols = integrals.shape[1]
    share = rows // X

    side = jnp.where((x % 2 == 0) == (c == 0), 1, -1)
    block = jnp.pad(amplitudes.reshape(X, share, depth), ((0, 0), (0, 16 - share), (0, 0)))
    block = jnp.concatenate(
        [lax.dynamic_index_in_dim(block, (x + side * k) % X, 0, keepdims=False) for k in range(X)], 0
    )
    f1 = send(block, along_y(1))
    h1 = send(block, along_y(-1))
    others = send(integrals, other_core)
    f2 = send(f1, along_y(1))
    h2 = send(h1, along_y(-1))

    def product(blocks, part):
        tall = jnp.concatenate(blocks, 0)
        out = jnp.dot(tall, part, precision=lax.Precision.HIGH, preferred_element_type=jnp.float32)
        return out.reshape(len(blocks), X, 16, cols)

    f3 = send(f2, along_y(1))
    h3 = send(h2, along_y(-1))
    near_blocks = (block, f1, h1, f2, h2)
    own = product(near_blocks, integrals)
    f3_after, own = lax.optimization_barrier((f3, own))
    f4 = send(f3_after, along_y(1))
    early = jnp.stack([own, product(near_blocks, others)], 1)
    h3_after, early = lax.optimization_barrier((h3, early))
    arrived = send(early[:, :, 1:3], along_x(1))
    passed_on = early[:, :, 3] + arrived[:, :, 1]
    far_blocks = (f3, h3_after, f4)
    late = jnp.stack([product(far_blocks, integrals), product(far_blocks, others)], 1)
    late_first = send(late[:, :, 1], along_x(1))
    late_last, late_far = late[:, :, 3], late[:, :, 2]
    first = early[:, :, 0] + arrived[:, :, 0] + send(passed_on, along_x(-1))
    second, first = lax.optimization_barrier((late[:, :, 0] + late_first, first))
    second = second + send(late_last, along_x(-1)) + send(late_far, along_x(2))
    pieces = jnp.stack(
        [first[0], first[3], second[2], first[4], first[1], first[2], second[0], second[1]], 1
    )
    pieces = pieces.reshape(2, 2, 4, 16, cols)

    at_home = z % 2 == c
    total = 0.0
    for near in (True, False):
        place = jnp.where(at_home, z if near else z + 2, z + 1 if near else z - 1) % 4
        odd = (place != (2 * y + c) % 4).astype(jnp.int32)
        for core in range(CORES):
            half = (jnp.where(at_home, 1 - core, core) != c).astype(jnp.int32)
            part = lax.dynamic_slice(pieces, (half, odd, 0, 0, 0), (1, 1, 4, 16, cols))
            total = total + send(part.reshape(4, 16, cols), to_window(near, core))
    spread = lax.all_to_all(total, AXES, 0, 0, tiled=True, axis_index_groups=classes())
    cycle_term = spread[0] + spread[1] + spread[2] + spread[3]
    cycle_term = cycle_term[:share]

    row_energy = (occupied_energy[None, :] - virtual_energy_rows[:, None]).reshape(-1)
    col_energy = (occupied_energy[None, :] - virtual_energy_cols[:, None]).reshape(-1)
    row_part = lax.dynamic_slice_in_dim(row_energy, wide * share, share)
    col_part = lax.dynamic_slice_in_dim(col_energy, narrow * cols, cols)
    return cycle_term / (row_part[:, None] + col_part[None, :])


def solution(mesh):
    in_specs = (P("narrow", "wide"), P("wide", "narrow"), P(), P(), P())
    out_specs = P("wide", "narrow")
    return jax.shard_map(
        per_device, mesh=mesh, in_specs=in_specs, out_specs=out_specs, check_vma=False
    )
```

```python
import jax
import jax.numpy as jnp
from jax import lax
from jax.sharding import PartitionSpec as P

Z, X, Y, CORES = 16, 4, 8, 2
AXES = ("wide", "narrow")
EVEN, ODD = (0, -2, -4, 2), (-1, 1, -3, 3)


def device(z, x, y, c):
    return (z % Z * X + x % X) * (Y * CORES) + y % Y * CORES + c


def table(move):
    return [
        (device(z, x, y, c), device(*move(z, x, y, c)))
        for z in range(Z)
        for x in range(X)
        for y in range(Y)
        for c in range(CORES)
    ]


def send(array, move):
    return lax.ppermute(array, AXES, table(move))


def other_core(z, x, y, c):
    return z, x, y, 1 - c


def along_y(step):
    return lambda z, x, y, c: (z, x, y + (step if c == 0 else -step), c)


def side_of(x, c):
    return 1 if (x % 2 == 0) == (c == 0) else -1


def along_x(step):
    return lambda z, x, y, c: (z, x + step * side_of(x, c), y, c)


def far_step(z):
    return z % 4 // 2 * 4 - 2


def to_window(near, core):
    def move(z, x, y, c):
        if z % 2 == c:
            return (z if near else z + far_step(z)), x, y, 1 - core
        return (z + 1 if near else z - 1), x, y, core

    return move


def lines_x():
    return [[device(z, x, y, c) for x in range(X)] for z in range(Z) for y in range(Y) for c in range(CORES)]


def classes():
    groups = []
    for r in range(4):
        c = r % 2
        for x in range(X):
            for y in range(Y):
                offsets = EVEN if (2 * y + c) % 4 == r else ODD
                places = [2 * (y + (o if c == 0 else -o)) + c for o in offsets]
                for core in range(CORES):
                    groups.append([device(z, x, y, core) for z in places])
    return groups


def per_device(amplitudes, integrals, occupied_energy, virtual_energy_rows, virtual_energy_cols):
    wide, narrow = lax.axis_index("wide"), lax.axis_index("narrow")
    z, x, y, c = wide // X, wide % X, narrow // CORES, narrow % CORES
    rows, depth = amplitudes.shape
    cols = integrals.shape[1]
    share = rows // X

    side = jnp.where((x % 2 == 0) == (c == 0), 1, -1)
    block = jnp.pad(amplitudes.reshape(X, share, depth), ((0, 0), (0, 16 - share), (0, 0)))
    block = block.reshape(X * 16, depth)
    f1 = send(block, along_y(1))
    h1 = send(block, along_y(-1))
    others = send(integrals, other_core)
    f2 = send(f1, along_y(1))
    h2 = send(h1, along_y(-1))

    def product(blocks, part):
        tall = jnp.concatenate(blocks, 0)
        out = jnp.dot(tall, part, precision=lax.Precision.HIGH, preferred_element_type=jnp.float32)
        return out.reshape(len(blocks), X, 16, cols)

    f3 = send(f2, along_y(1))
    h3 = send(h2, along_y(-1))
    near_blocks = (block, f1, h1, f2, h2)
    own = product(near_blocks, integrals)
    f3_after, own = lax.optimization_barrier((f3, own))
    f4 = send(f3_after, along_y(1))
    early = jnp.stack([own, product(near_blocks, others)], 1)
    h3_after, early = lax.optimization_barrier((h3, early))

    def place(k):
        return lax.dynamic_index_in_dim(early, (x + side * k) % X, 2, keepdims=False)

    arrived = send(jnp.stack([place(1), place(2)], 0), along_x(1))
    passed_on = place(3) + arrived[1]
    far_blocks = (f3, h3_after, f4)
    late = jnp.stack([product(far_blocks, integrals), product(far_blocks, others)], 1)
    late = late.transpose(2, 0, 1, 3, 4)
    first = place(0) + arrived[0] + send(passed_on, along_x(-1))
    second = lax.all_to_all(late, AXES, 0, 0, tiled=True, axis_index_groups=lines_x())
    second = second[0] + second[1] + second[2] + second[3]
    pieces = jnp.stack(
        [first[0], first[3], second[2], first[4], first[1], first[2], second[0], second[1]], 1
    )
    pieces = pieces.reshape(2, 2, 4, 16, cols)

    at_home = z % 2 == c
    total = 0.0
    for near in (True, False):
        place = jnp.where(at_home, z if near else z + 2, z + 1 if near else z - 1) % 4
        odd = (place != (2 * y + c) % 4).astype(jnp.int32)
        for core in range(CORES):
            half = (jnp.where(at_home, 1 - core, core) != c).astype(jnp.int32)
            part = lax.dynamic_slice(pieces, (half, odd, 0, 0, 0), (1, 1, 4, 16, cols))
            total = total + send(part.reshape(4, 16, cols), to_window(near, core))
    spread = lax.all_to_all(total, AXES, 0, 0, tiled=True, axis_index_groups=classes())
    cycle_term = spread[0] + spread[1] + spread[2] + spread[3]
    cycle_term = cycle_term[:share]

    row_energy = (occupied_energy[None, :] - virtual_energy_rows[:, None]).reshape(-1)
    col_energy = (occupied_energy[None, :] - virtual_energy_cols[:, None]).reshape(-1)
    row_part = lax.dynamic_slice_in_dim(row_energy, wide * share, share)
    col_part = lax.dynamic_slice_in_dim(col_energy, narrow * cols, cols)
    return cycle_term / (row_part[:, None] + col_part[None, :])


def solution(mesh):
    in_specs = (P("narrow", "wide"), P("wide", "narrow"), P(), P(), P())
    out_specs = P("wide", "narrow")
    return jax.shard_map(
        per_device, mesh=mesh, in_specs=in_specs, out_specs=out_specs, check_vma=False
    )
```

```python
import jax
import jax.numpy as jnp
from jax import lax
from jax.sharding import PartitionSpec as P

Z, X, Y, CORES = 16, 4, 8, 2
AXES = ("wide", "narrow")
EVEN, ODD = (0, -2, -4, 2), (-1, 1, -3, 3)


def device(z, x, y, c):
    return (z % Z * X + x % X) * (Y * CORES) + y % Y * CORES + c


def table(move):
    return [
        (device(z, x, y, c), device(*move(z, x, y, c)))
        for z in range(Z)
        for x in range(X)
        for y in range(Y)
        for c in range(CORES)
    ]


def send(array, move):
    return lax.ppermute(array, AXES, table(move))


def other_core(z, x, y, c):
    return z, x, y, 1 - c


def along_y(step):
    return lambda z, x, y, c: (z, x, y + (step if c == 0 else -step), c)


def side_of(x, c):
    return 1 if (x % 2 == 0) == (c == 0) else -1


def along_x(step):
    return lambda z, x, y, c: (z, x + step * side_of(x, c), y, c)


def far_step(z):
    return z % 4 // 2 * 4 - 2


def to_window(near, core):
    def move(z, x, y, c):
        if z % 2 == c:
            return (z if near else z + far_step(z)), x, y, 1 - core
        return (z + 1 if near else z - 1), x, y, core

    return move


def lines_x():
    return [[device(z, x, y, c) for x in range(X)] for z in range(Z) for y in range(Y) for c in range(CORES)]


def classes():
    groups = []
    for r in range(4):
        c = r % 2
        for x in range(X):
            for y in range(Y):
                offsets = EVEN if (2 * y + c) % 4 == r else ODD
                places = [2 * (y + (o if c == 0 else -o)) + c for o in offsets]
                for core in range(CORES):
                    groups.append([device(z, x, y, core) for z in places])
    return groups


def per_device(amplitudes, integrals, occupied_energy, virtual_energy_rows, virtual_energy_cols):
    wide, narrow = lax.axis_index("wide"), lax.axis_index("narrow")
    z, x, y, c = wide // X, wide % X, narrow // CORES, narrow % CORES
    rows, depth = amplitudes.shape
    cols = integrals.shape[1]
    share = rows // X

    side = jnp.where((x % 2 == 0) == (c == 0), 1, -1)
    block = jnp.pad(amplitudes.reshape(X, share, depth), ((0, 0), (0, 16 - share), (0, 0)))
    block = block.reshape(X * 16, depth)
    f1 = send(block, along_y(1))
    h1 = send(block, along_y(-1))
    others = send(integrals, other_core)
    f2 = send(f1, along_y(1))
    h2 = send(h1, along_y(-1))

    def product(blocks, part):
        tall = jnp.concatenate(blocks, 0)
        out = jnp.dot(tall, part, precision=lax.Precision.HIGH, preferred_element_type=jnp.float32)
        return out.reshape(len(blocks), X, 16, cols)

    f3 = send(f2, along_y(1))
    h3 = send(h2, along_y(-1))
    near_blocks = (block, f1, h1, f2, h2)
    own = product(near_blocks, integrals)
    early = jnp.stack([own, product(near_blocks, others)], 1)
    f3_after, early = lax.optimization_barrier((f3, early))
    f4 = send(f3_after, along_y(1))

    def place(k):
        return lax.dynamic_index_in_dim(early, (x + side * k) % X, 2, keepdims=False)

    arrived = send(jnp.stack([place(1), place(2)], 0), along_x(1))
    passed_on = place(3) + arrived[1]
    far_blocks = (f3, h3, f4)
    late = jnp.stack([product(far_blocks, integrals), product(far_blocks, others)], 1)
    late = late.transpose(2, 0, 1, 3, 4)
    first = place(0) + arrived[0] + send(passed_on, along_x(-1))
    second = lax.all_to_all(late, AXES, 0, 0, tiled=True, axis_index_groups=lines_x())
    second = second[0] + second[1] + second[2] + second[3]
    pieces = jnp.stack(
        [first[0], first[3], second[2], first[4], first[1], first[2], second[0], second[1]], 1
    )
    pieces = pieces.reshape(2, 2, 4, 16, cols)

    at_home = z % 2 == c
    total = 0.0
    for near in (True, False):
        place = jnp.where(at_home, z if near else z + 2, z + 1 if near else z - 1) % 4
        odd = (place != (2 * y + c) % 4).astype(jnp.int32)
        for core in range(CORES):
            half = (jnp.where(at_home, 1 - core, core) != c).astype(jnp.int32)
            part = lax.dynamic_slice(pieces, (half, odd, 0, 0, 0), (1, 1, 4, 16, cols))
            total = total + send(part.reshape(4, 16, cols), to_window(near, core))
    spread = lax.all_to_all(total, AXES, 0, 0, tiled=True, axis_index_groups=classes())
    cycle_term = spread[0] + spread[1] + spread[2] + spread[3]
    cycle_term = cycle_term[:share]

    row_energy = (occupied_energy[None, :] - virtual_energy_rows[:, None]).reshape(-1)
    col_energy = (occupied_energy[None, :] - virtual_energy_cols[:, None]).reshape(-1)
    row_part = lax.dynamic_slice_in_dim(row_energy, wide * share, share)
    col_part = lax.dynamic_slice_in_dim(col_energy, narrow * cols, cols)
    return cycle_term / (row_part[:, None] + col_part[None, :])


def solution(mesh):
    in_specs = (P("narrow", "wide"), P("wide", "narrow"), P(), P(), P())
    out_specs = P("wide", "narrow")
    return jax.shard_map(
        per_device, mesh=mesh, in_specs=in_specs, out_specs=out_specs, check_vma=False
    )
```

```python
import jax
import jax.numpy as jnp
from jax import lax
from jax.sharding import PartitionSpec as P

Z, X, Y, CORES = 16, 4, 8, 2
AXES = ("wide", "narrow")
EVEN, ODD = (0, -2, -4, 2), (-1, 1, -3, 3)


def device(z, x, y, c):
    return (z % Z * X + x % X) * (Y * CORES) + y % Y * CORES + c


def table(move):
    return [
        (device(z, x, y, c), device(*move(z, x, y, c)))
        for z in range(Z)
        for x in range(X)
        for y in range(Y)
        for c in range(CORES)
    ]


def send(array, move):
    return lax.ppermute(array, AXES, table(move))


def other_core(z, x, y, c):
    return z, x, y, 1 - c


def along_y(step):
    return lambda z, x, y, c: (z, x, y + (step if c == 0 else -step), c)


def side_of(x, c):
    return 1 if (x % 2 == 0) == (c == 0) else -1


def along_x(step):
    return lambda z, x, y, c: (z, x + step * side_of(x, c), y, c)


def far_step(z):
    return z % 4 // 2 * 4 - 2


def to_window(near, core):
    def move(z, x, y, c):
        if z % 2 == c:
            return (z if near else z + far_step(z)), x, y, 1 - core
        return (z + 1 if near else z - 1), x, y, core

    return move


def classes():
    groups = []
    for r in range(4):
        c = r % 2
        for x in range(X):
            for y in range(Y):
                offsets = EVEN if (2 * y + c) % 4 == r else ODD
                places = [2 * (y + (o if c == 0 else -o)) + c for o in offsets]
                for core in range(CORES):
                    groups.append([device(z, x, y, core) for z in places])
    return groups


def per_device(amplitudes, integrals, occupied_energy, virtual_energy_rows, virtual_energy_cols):
    wide, narrow = lax.axis_index("wide"), lax.axis_index("narrow")
    z, x, y, c = wide // X, wide % X, narrow // CORES, narrow % CORES
    rows, depth = amplitudes.shape
    cols = integrals.shape[1]
    share = rows // X

    side = jnp.where((x % 2 == 0) == (c == 0), 1, -1)
    block = jnp.pad(amplitudes.reshape(X, share, depth), ((0, 0), (0, 16 - share), (0, 0)))
    block = jnp.concatenate(
        [lax.dynamic_index_in_dim(block, (x + side * k) % X, 0, keepdims=False) for k in range(X)], 0
    )
    f1 = send(block, along_y(1))
    h1 = send(block, along_y(-1))
    others = send(integrals, other_core)
    f2 = send(f1, along_y(1))
    h2 = send(h1, along_y(-1))

    def product(blocks, part):
        tall = jnp.concatenate(blocks, 0)
        out = jnp.dot(tall, part, precision=lax.Precision.HIGH, preferred_element_type=jnp.float32)
        return out.reshape(len(blocks), X, 16, cols)

    f3 = send(f2, along_y(1))
    h3 = send(h2, along_y(-1))
    near_blocks = (block, f1, h1, f2, h2)
    own = product(near_blocks, integrals)
    f3_after, own = lax.optimization_barrier((f3, own))
    f4 = send(f3_after, along_y(1))
    early = jnp.stack([own, product(near_blocks, others)], 1)
    h3_after, early = lax.optimization_barrier((h3, early))
    arrived = send(early[:, :, 1:3], along_x(1))
    passed_on = early[:, :, 3] + arrived[:, :, 1]
    far_blocks = (f3, h3_after, f4)
    late = jnp.stack([product(far_blocks, integrals), product(far_blocks, others)], 1)
    late_arrived = send(late[:, :, 1:3], along_x(1))
    late_passed_on = late[:, :, 3] + late_arrived[:, :, 1]
    summed = send(jnp.concatenate([passed_on, late_passed_on], 0), along_x(-1))
    summed = summed + jnp.concatenate([early[:, :, 0] + arrived[:, :, 0], late[:, :, 0] + late_arrived[:, :, 0]], 0)
    pieces = jnp.stack(
        [summed[k] for k in (0, 3, 7, 4, 1, 2, 5, 6)], 1
    )
    pieces = pieces.reshape(2, 2, 4, 16, cols)

    at_home = z % 2 == c
    total = 0.0
    for near in (True, False):
        place = jnp.where(at_home, z if near else z + 2, z + 1 if near else z - 1) % 4
        odd = (place != (2 * y + c) % 4).astype(jnp.int32)
        for core in range(CORES):
            half = (jnp.where(at_home, 1 - core, core) != c).astype(jnp.int32)
            part = lax.dynamic_slice(pieces, (half, odd, 0, 0, 0), (1, 1, 4, 16, cols))
            total = total + send(part.reshape(4, 16, cols), to_window(near, core))
    spread = lax.all_to_all(total, AXES, 0, 0, tiled=True, axis_index_groups=classes())
    cycle_term = spread[0] + spread[1] + spread[2] + spread[3]
    cycle_term = cycle_term[:share]

    row_energy = (occupied_energy[None, :] - virtual_energy_rows[:, None]).reshape(-1)
    col_energy = (occupied_energy[None, :] - virtual_energy_cols[:, None]).reshape(-1)
    row_part = lax.dynamic_slice_in_dim(row_energy, wide * share, share)
    col_part = lax.dynamic_slice_in_dim(col_energy, narrow * cols, cols)
    return cycle_term / (row_part[:, None] + col_part[None, :])


def solution(mesh):
    in_specs = (P("narrow", "wide"), P("wide", "narrow"), P(), P(), P())
    out_specs = P("wide", "narrow")
    return jax.shard_map(
        per_device, mesh=mesh, in_specs=in_specs, out_specs=out_specs, check_vma=False
    )
```

```python
import jax
import jax.numpy as jnp
from jax import lax
from jax.sharding import PartitionSpec as P

Z, X, Y, CORES = 16, 4, 8, 2
AXES = ("wide", "narrow")
EVEN, ODD = (0, -2, -4, 2), (-1, 1, -3, 3)


def device(z, x, y, c):
    return (z % Z * X + x % X) * (Y * CORES) + y % Y * CORES + c


def table(move):
    return [
        (device(z, x, y, c), device(*move(z, x, y, c)))
        for z in range(Z)
        for x in range(X)
        for y in range(Y)
        for c in range(CORES)
    ]


def send(array, move):
    return lax.ppermute(array, AXES, table(move))


def other_core(z, x, y, c):
    return z, x, y, 1 - c


def along_y(step):
    return lambda z, x, y, c: (z, x, y + (step if c == 0 else -step), c)


def side_of(x, c):
    return 1 if (x % 2 == 0) == (c == 0) else -1


def along_x(step):
    return lambda z, x, y, c: (z, x + step * side_of(x, c), y, c)


def far_step(z):
    return z % 4 // 2 * 4 - 2


def to_window(near, core):
    def move(z, x, y, c):
        if z % 2 == c:
            return (z if near else z + far_step(z)), x, y, 1 - core
        return (z + 1 if near else z - 1), x, y, core

    return move


def classes():
    groups = []
    for r in range(4):
        c = r % 2
        for x in range(X):
            for y in range(Y):
                offsets = EVEN if (2 * y + c) % 4 == r else ODD
                places = [2 * (y + (o if c == 0 else -o)) + c for o in offsets]
                for core in range(CORES):
                    groups.append([device(z, x, y, core) for z in places])
    return groups


def per_device(amplitudes, integrals, occupied_energy, virtual_energy_rows, virtual_energy_cols):
    wide, narrow = lax.axis_index("wide"), lax.axis_index("narrow")
    z, x, y, c = wide // X, wide % X, narrow // CORES, narrow % CORES
    rows, depth = amplitudes.shape
    cols = integrals.shape[1]
    share = rows // X

    side = jnp.where((x % 2 == 0) == (c == 0), 1, -1)
    block = jnp.pad(amplitudes.reshape(X, share, depth), ((0, 0), (0, 16 - share), (0, 0)))
    block = jnp.concatenate(
        [lax.dynamic_index_in_dim(block, (x + side * k) % X, 0, keepdims=False) for k in range(X)], 0
    )
    f1 = send(block, along_y(1))
    h1 = send(block, along_y(-1))
    others = send(integrals, other_core)
    f2 = send(f1, along_y(1))
    h2 = send(h1, along_y(-1))

    def product(blocks, part):
        tall = jnp.concatenate(blocks, 0)
        out = jnp.dot(tall, part, precision=lax.Precision.HIGH, preferred_element_type=jnp.float32)
        return out.reshape(len(blocks), X, 16, cols)

    f3 = send(f2, along_y(1))
    h3 = send(h2, along_y(-1))
    near_blocks = (block, f1, h1, f2, h2)
    early = jnp.stack([product(near_blocks, integrals), product(near_blocks, others)], 1)
    f3_after, early = lax.optimization_barrier((f3, early))
    f4 = send(f3_after, along_y(1))
    arrived = send(early[:, :, 1:3], along_x(1))
    passed_on = early[:, :, 3] + arrived[:, :, 1]
    far_blocks = (f3, h3, f4)
    late = jnp.stack([product(far_blocks, integrals), product(far_blocks, others)], 1)
    late_first = send(late[:, :, 1], along_x(1))
    late_last, late_far = late[:, :, 3], late[:, :, 2]
    first = early[:, :, 0] + arrived[:, :, 0] + send(passed_on, along_x(-1))
    second, first = lax.optimization_barrier((late[:, :, 0] + late_first, first))
    second = second + send(late_last, along_x(-1)) + send(late_far, along_x(2))
    pieces = jnp.stack(
        [first[0], first[3], second[2], first[4], first[1], first[2], second[0], second[1]], 1
    )
    pieces = pieces.reshape(2, 2, 4, 16, cols)

    at_home = z % 2 == c
    total = 0.0
    for near in (True, False):
        place = jnp.where(at_home, z if near else z + 2, z + 1 if near else z - 1) % 4
        odd = (place != (2 * y + c) % 4).astype(jnp.int32)
        for core in range(CORES):
            half = (jnp.where(at_home, 1 - core, core) != c).astype(jnp.int32)
            part = lax.dynamic_slice(pieces, (half, odd, 0, 0, 0), (1, 1, 4, 16, cols))
            total = total + send(part.reshape(4, 16, cols), to_window(near, core))
    spread = lax.all_to_all(total, AXES, 0, 0, tiled=True, axis_index_groups=classes())
    cycle_term = spread[0] + spread[1] + spread[2] + spread[3]
    cycle_term = cycle_term[:share]

    row_energy = (occupied_energy[None, :] - virtual_energy_rows[:, None]).reshape(-1)
    col_energy = (occupied_energy[None, :] - virtual_energy_cols[:, None]).reshape(-1)
    row_part = lax.dynamic_slice_in_dim(row_energy, wide * share, share)
    col_part = lax.dynamic_slice_in_dim(col_energy, narrow * cols, cols)
    return cycle_term / (row_part[:, None] + col_part[None, :])


def solution(mesh):
    in_specs = (P("narrow", "wide"), P("wide", "narrow"), P(), P(), P())
    out_specs = P("wide", "narrow")
    return jax.shard_map(
        per_device, mesh=mesh, in_specs=in_specs, out_specs=out_specs, check_vma=False
    )
```
